32 devices in a mesh: delay: 8 (over z, y), row: 2 (over core), col: 2 (over x).
Axes of the slice: x: 2, y: 2, z: 4, core: 2. Of those that a mesh axis runs over, the one named last changes fastest.
Arguments:
- delays: float32 [8, 4096, 2, 2048], P('delay', 'row', None, 'col'), may hold values from -0.015625 to 0.015625
- history: float32 [8, 256, 4096], P('delay', None, ('row', 'col')), may hold values from -6 to 6
- sources: float32 [4, 256, 4096], P(None, None, ('row', 'col')), may hold values from -6 to 6
- self_inverse: float32 [16, 256, 256], P(('row', 'col')), may hold values from -4 to 4, as said below
Outputs:
- adjoints: float32 [4, 256, 4096], P(None, None, ('row', 'col'))
The draws below stay inside these ranges and needn't reach their ends.
Inputs may be any that keep to these rules, and one draw needn't show every extreme that they name: `self_inverse`: dense blocks.
All inputs are finite; a program needn't handle non-finite values.
Results may differ from the reference program's by a relative error of at most 0.0001.
Values sent between devices are 32-bit elements; how exact they have to be, the bound alone decides.
A program may use at most 128 MiB of HBM per device.

```python
import jax
import jax.numpy as jnp
from jax import lax

N = 4096
R = 256
S = 256
STEPS = 4
K = 8
BLOCKS = 16
N_ROW = 2


def draw_self_inverse(key, part):
    noise = jax.random.normal(jax.random.fold_in(key, 11), (N // S, S, S), jnp.float32)
    blocks = jnp.eye(S, dtype=jnp.float32)[None] + 0.6 * noise / jnp.sqrt(jnp.float32(S))
    return jnp.clip(blocks, -4.0, 4.0)


def level_of(rng, dims, split, smallest, largest):
    def one(dim, shards_of):
        draws = jax.random.uniform(jax.random.fold_in(jax.random.fold_in(rng, 6), dim), (shards_of,), jnp.float32, smallest / len(split), largest / len(split))
        return jnp.repeat(jnp.exp(draws), dims[dim] // shards_of).reshape((-1,) + (1,) * (len(dims) - dim - 1))

    factor_of = one(*split[0])
    for cut in split[1:]:
        factor_of = factor_of * one(*cut)
    return factor_of


def scatter_about(rng, shape, spread, bound, shards=(), held_as=jnp.bfloat16):
    level = level_of(rng, shape, shards, -0.22, 0.18) if shards else 1.0
    values = jax.random.normal(rng, shape, jnp.float32) * spread * level
    return jnp.minimum(jnp.maximum(values, -bound), bound).astype(held_as)


def setup_inputs(seed: int = 0) -> dict:
    keys = jax.random.split(jax.random.key(seed), 5)
    return {
        "delays": scatter_about(keys[0], (K, N, N_ROW, N // N_ROW), (4 * N * K) ** -0.5, 0.015625, ((0, 8), (1, 2), (3, 2)), jnp.float32),
        "history": scatter_about(keys[1], (K, R, N), 1.0, 6.0, ((0, 8), (2, 4)), jnp.float32),
        "sources": scatter_about(keys[2], (STEPS, R, N), 1.0, 6.0, ((2, 4),), jnp.float32),
        "self_inverse": draw_self_inverse(jax.random.fold_in(keys[4], 71), 0),
    }


def reference(delays, history, sources, self_inverse):
    mats = delays.reshape(K, N, N)
    highest = lax.Precision.HIGHEST

    def add_delay(total, pair):
        hist_k, mat_k = pair
        return total + jnp.einsum("rj,ij->ri", hist_k, mat_k, precision=highest), None

    def one_step(hist, source):
        coupled, unused = lax.scan(add_delay, jnp.zeros((R, N), jnp.float32), (hist, mats))
        drive = (source - coupled).reshape(R, BLOCKS, S)
        adjoint = jnp.einsum("rbs,bst->rbt", drive, self_inverse, precision=highest).reshape(R, N)
        hist = jnp.concatenate([adjoint[None], hist[:-1]], axis=0)
        return hist, adjoint

    final, adjoints = lax.scan(one_step, history, sources)
    return adjoints
```

```python
import functools

import jax
import jax.numpy as jnp
from jax import lax
from jax.experimental import pallas as pl
from jax.experimental.pallas import tpu as pltpu
from jax.sharding import PartitionSpec as P

MESH = pl.DeviceIdType.MESH
GROUPS = 2


def split_two(x):
    high = x.astype(jnp.bfloat16)
    low = (x - high.astype(jnp.float32)).astype(jnp.bfloat16)
    return high, low


def times_transposed(a, b):
    return lax.dot_general(a, b, (((1,), (1,)), ((), ())), preferred_element_type=jnp.float32)


def kernel(
    sizes, m_high, m_low, hist, sources, inverse, out,
    xs, partner, older, p_send, p_recv, total, z_recv, y_recv,
    x_send_sem, x_recv_sem, z_send_sem, z_recv_sem, y_recv_sem,
    b_one_sem, b_two_sem, b_recv_sem, r_send_sem, r_recv_sem, h_send_sem, h_recv_sem,
):
    n_delay, n_col, steps, rows, blocks, order = sizes
    items = steps * GROUPS
    part = rows // GROUPS
    width = blocks * order
    k = lax.axis_index("delay")
    r = lax.axis_index("row")
    c = lax.axis_index("col")
    has_one = k + 1 < n_delay
    has_two = k + 2 < n_delay

    def remote(src, dst, send, recv, **where):
        return pltpu.make_async_remote_copy(
            src_ref=src, dst_ref=dst, send_sem=send, recv_sem=recv,
            device_id=where, device_id_type=MESH,
        )

    def arrived(ref, sem):
        remote(ref, ref, sem, sem, row=1 - r).wait_recv()

    def col_at(by):
        return lax.rem(c + by, n_col)

    barrier = pltpu.get_barrier_semaphore()

    def greet(**where):
        pl.semaphore_signal(barrier, inc=1, device_id=where, device_id_type=MESH)

    greet(row=1 - r)
    for by in range(1, n_col):
        greet(col=col_at(by))
    pl.when(has_one)(lambda: greet(delay=k + 1))
    pl.when(has_two)(lambda: greet(delay=k + 2))
    pl.when(k >= 1)(lambda: greet(delay=k - 1))
    pl.when(k >= 2)(lambda: greet(delay=k - 2))
    peers = n_col
    for there in (has_one, has_two, k >= 1, k >= 2):
        peers = peers + jnp.where(there, 1, 0)
    pl.semaphore_wait(barrier, peers)

    def rows_of(g):
        return pl.ds(pl.multiple_of(g * part, part), part)

    def cell(s, g, b):
        return out.at[s, rows_of(g), pl.ds(pl.multiple_of(b * order, order), order)]

    def older_copy(src, j, g, by):
        return remote(src, older.at[j, rows_of(g)], h_send_sem.at[j, g], h_recv_sem.at[j, g], delay=k + by)

    def put(half, value):
        high, low = split_two(value)
        xs[half, pl.ds(0, part)] = high
        xs[half, pl.ds(part, part)] = low

    def to_partner(src, n):
        return remote(src, partner.at[n], r_send_sem.at[n], r_recv_sem.at[n], row=1 - r)

    def tile(first):
        at = pl.ds(pl.multiple_of(first, order), order)
        acc = jnp.zeros((part, order), jnp.float32)
        for h in range(2):
            high = m_high[at, h * width:(h + 1) * width]
            low = m_low[at, h * width:(h + 1) * width]
            both = times_transposed(xs[h], high)
            acc = acc + (both[:part] + both[part:] + times_transposed(xs[h, :part], low))
        return acc

    def p_copy(n, by, b):
        return remote(
            p_send.at[n, by - 1, b], p_recv.at[n, by - 1, b],
            x_send_sem.at[n, by - 1], x_recv_sem.at[n, by - 1, b], col=col_at(by),
        )

    def multiply(n):
        s, g = n // GROUPS, n % GROUPS

        @pl.when(s == 0)
        def _():
            to_partner(hist.at[rows_of(g)], n).start()
            pl.when(has_one)(lambda: older_copy(hist.at[rows_of(g)], 0, g, 1).start())
            put(r, hist[rows_of(g)])

        @pl.when((s >= 1) & (k >= s))
        def _():
            arrived(older.at[s - 1, rows_of(g)], h_recv_sem.at[s - 1, g])
            to_partner(older.at[s - 1, rows_of(g)], n).start()
            if steps > 3:
                @pl.when((s == 1) & has_two)
                def _():
                    older_copy(older.at[0, rows_of(g)], 2, g, 2).start()
            put(r, older[s - 1, rows_of(g)])

        @pl.when((s >= 1) & (k < s))
        def _():
            to_partner(out.at[s - 1 - k, rows_of(g)], n).start()
            put(r, out[s - 1 - k, rows_of(g)])

        arrived(partner.at[n], r_recv_sem.at[n])
        put(1 - r, partner[n])

        for by in range(1, n_col):
            def far(b, carry):
                p_send[n, by - 1, b] = tile((col_at(by) * blocks + b) * order)
                p_copy(n, by, b).start()
                return carry

            lax.fori_loop(0, blocks, far, 0)

        def near(b, carry):
            total[n, b] = tile((c * blocks + b) * order)
            return carry

        lax.fori_loop(0, blocks, near, 0)

        @pl.when((s == 0) & has_two)
        def _():
            older_copy(hist.at[rows_of(g)], 1, g, 2).start()

    def z_copy(n, b):
        return remote(total.at[n, b], z_recv.at[n, b], z_send_sem.at[n], z_recv_sem.at[n, b], delay=k - 2)

    def y_copy(n, b):
        return remote(total.at[n, b], y_recv.at[n, b], z_send_sem.at[n], y_recv_sem.at[n, b], delay=k - 1)

    def b_copy(n, b, by, sem):
        s, g = n // GROUPS, n % GROUPS
        return remote(cell(s, g, b), cell(s, g, b), sem.at[n], b_recv_sem.at[n, b], delay=k + by)

    def reduce(n):
        s, g = n // GROUPS, n % GROUPS

        def one(b, carry):
            value = total[n, b]
            for by in range(1, n_col):
                arrived(p_recv.at[n, by - 1, b], x_recv_sem.at[n, by - 1, b])
                value = value + p_recv[n, by - 1, b]
            total[n, b] = value

            @pl.when(has_two)
            def _():
                arrived(z_recv.at[n, b], z_recv_sem.at[n, b])
                total[n, b] = total[n, b] + z_recv[n, b]

            pl.when(k >= 2)(lambda: z_copy(n, b).start())
            pl.when(k == 1)(lambda: y_copy(n, b).start())

            @pl.when(k == 0)
            def _():
                arrived(y_recv.at[n, b], y_recv_sem.at[n, b])
                at = pl.ds(pl.multiple_of(b * order, order), order)
                drive = sources[s, rows_of(g), at] - (total[n, b] + y_recv[n, b])
                out[s, rows_of(g), at] = jnp.dot(
                    drive, inverse[b], precision=lax.Precision.HIGHEST,
                    preferred_element_type=jnp.float32,
                )
                b_copy(n, b, 1, b_one_sem).start()
                if n_delay > 2:
                    b_copy(n, b, 2, b_two_sem).start()

            return carry

        lax.fori_loop(0, blocks, one, 0)

    def pass_on(n):
        s, g = n // GROUPS, n % GROUPS

        def one(b, carry):
            arrived(cell(s, g, b), b_recv_sem.at[n, b])
            pl.when(has_two)(lambda: b_copy(n, b, 2, b_two_sem).start())
            return carry

        @pl.when(k >= 1)
        def _():
            lax.fori_loop(0, blocks, one, 0)

    def turn(i, carry):
        pl.when((i >= GROUPS) & (i < items + GROUPS))(lambda: reduce(i - GROUPS))
        pl.when(i >= 2 * GROUPS)(lambda: pass_on(i - 2 * GROUPS))
        pl.when(i < items)(lambda: multiply(i))
        return carry

    lax.fori_loop(0, items + 2 * GROUPS, turn, 0)

    def whole_send(ref, sem):
        remote(ref, ref, sem, sem, row=1 - r).wait_send()

    def settle(n, carry):
        s, g = n // GROUPS, n % GROUPS
        for by in range(1, n_col):
            whole_send(p_send.at[n, by - 1], x_send_sem.at[n, by - 1])
        whole_send(partner.at[n], r_send_sem.at[n])
        pl.when(k >= 1)(lambda: whole_send(total.at[n], z_send_sem.at[n]))
        pl.when(k == 0)(lambda: whole_send(out.at[s, rows_of(g)], b_one_sem.at[n]))
        pl.when(has_two)(lambda: whole_send(out.at[s, rows_of(g)], b_two_sem.at[n]))
        return carry

    lax.fori_loop(0, items, settle, 0)
    for g in range(GROUPS):
        pl.when(has_one)(lambda: whole_send(partner.at[0], h_send_sem.at[0, g]))
        pl.when(has_two)(lambda: whole_send(partner.at[0], h_send_sem.at[1, g]))
        pl.when((k >= 1) & has_two)(lambda: whole_send(partner.at[0], h_send_sem.at[2, g]))


def on_device(n_delay, n_col, delays, history, sources, self_inverse):
    out_rows = delays.shape[1]
    tiles = delays.reshape(out_rows, -1)
    rounded = lax.reduce_precision(tiles, 8, 7)
    m_high = rounded.astype(jnp.bfloat16)
    m_low = (tiles - rounded).astype(jnp.bfloat16)
    steps, rows, width = sources.shape
    blocks, order, _ = self_inverse.shape
    items, part = steps * GROUPS, rows // GROUPS
    sizes = (n_delay, n_col, steps, rows, blocks, order)
    dma = pltpu.SemaphoreType.DMA
    f32 = jnp.float32
    far = n_col - 1
    cells = (items, blocks, part, order)
    return pl.pallas_call(
        functools.partial(kernel, sizes),
        out_shape=jax.ShapeDtypeStruct(sources.shape, f32),
        in_specs=[pl.BlockSpec(memory_space=pltpu.VMEM)] * 5,
        out_specs=pl.BlockSpec(memory_space=pltpu.VMEM),
        scratch_shapes=[
            pltpu.VMEM((2, 2 * part, width), jnp.bfloat16),
            pltpu.VMEM((items, part, width), f32),
            pltpu.VMEM((steps - 1, rows, width), f32),
            pltpu.VMEM((items, far, blocks, part, order), f32),
            pltpu.VMEM((items, far, blocks, part, order), f32),
            pltpu.VMEM(cells, f32),
            pltpu.VMEM(cells, f32),
            pltpu.VMEM(cells, f32),
            dma((items, far)),
            dma((items, far, blocks)),
            dma((items,)),
            dma((items, blocks)),
            dma((items, blocks)),
            dma((items,)),
            dma((items,)),
            dma((items, blocks)),
            dma((items,)),
            dma((items,)),
            dma((steps - 1, GROUPS)),
            dma((steps - 1, GROUPS)),
        ],
        compiler_params=pltpu.CompilerParams(
            collective_id=0, has_side_effects=True, vmem_limit_bytes=60 * 2**20
        ),
        cost_estimate=pl.CostEstimate(
            flops=6 * steps * rows * out_rows * tiles.shape[1], bytes_accessed=24 * 2**20, transcendentals=0
        ),
    )(m_high, m_low, history[0], sources, self_inverse)


def solution(mesh):
    placed = (
        P("delay", "row", None, "col"),
        P("delay", None, ("row", "col")),
        P(None, None, ("row", "col")),
        P(("row", "col"), None, None),
    )
    return jax.shard_map(
        functools.partial(on_device, mesh.shape["delay"], mesh.shape["col"]),
        mesh=mesh,
        in_specs=placed,
        out_specs=P(None, None, ("row", "col")),
        check_vma=False,
    )
```

```python
import functools

import jax
import jax.numpy as jnp
from jax import lax
from jax.experimental import pallas as pl
from jax.experimental.pallas import tpu as pltpu
from jax.sharding import PartitionSpec as P

MESH = pl.DeviceIdType.MESH
GROUPS = 2


def split_two(x):
    high = x.astype(jnp.bfloat16)
    low = (x - high.astype(jnp.float32)).astype(jnp.bfloat16)
    return high, low


def times(a, b):
    return jnp.dot(a, b, preferred_element_type=jnp.float32)


def kernel(
    sizes, high_0, high_1, low_0, low_1, hist, sources, inverse, out,
    xs, partner, older, p_send, p_recv, total, z_recv, y_recv,
    x_send_sem, x_recv_sem, z_send_sem, z_recv_sem, y_recv_sem,
    b_one_sem, b_two_sem, b_recv_sem, r_send_sem, r_recv_sem, h_send_sem, h_recv_sem,
):
    n_delay, n_col, steps, rows, blocks, order = sizes
    items = steps * GROUPS
    part = rows // GROUPS
    width = blocks * order
    k = lax.axis_index("delay")
    r = lax.axis_index("row")
    c = lax.axis_index("col")
    has_one = k + 1 < n_delay
    has_two = k + 2 < n_delay

    def remote(src, dst, send, recv, **where):
        return pltpu.make_async_remote_copy(
            src_ref=src, dst_ref=dst, send_sem=send, recv_sem=recv,
            device_id=where, device_id_type=MESH,
        )

    def arrived(ref, sem):
        remote(ref, ref, sem, sem, row=1 - r).wait_recv()

    def col_at(by):
        return lax.rem(c + by, n_col)

    barrier = pltpu.get_barrier_semaphore()

    def greet(**where):
        pl.semaphore_signal(barrier, inc=1, device_id=where, device_id_type=MESH)

    greet(row=1 - r)
    for by in range(1, n_col):
        greet(col=col_at(by))
    pl.when(has_one)(lambda: greet(delay=k + 1))
    pl.when(has_two)(lambda: greet(delay=k + 2))
    pl.when(k >= 1)(lambda: greet(delay=k - 1))
    pl.when(k >= 2)(lambda: greet(delay=k - 2))
    peers = n_col
    for there in (has_one, has_two, k >= 1, k >= 2):
        peers = peers + jnp.where(there, 1, 0)
    pl.semaphore_wait(barrier, peers)

    def rows_of(g):
        return pl.ds(pl.multiple_of(g * part, part), part)

    def cell(s, g, b):
        return out.at[s, rows_of(g), pl.ds(pl.multiple_of(b * order, order), order)]

    def older_copy(src, j, g, by):
        return remote(src, older.at[j, rows_of(g)], h_send_sem.at[j, g], h_recv_sem.at[j, g], delay=k + by)

    def put(half, value):
        high, low = split_two(value.T)
        xs[half, :, :part] = high
        xs[half, :, part:] = low

    def to_partner(src, n):
        return remote(src, partner.at[n], r_send_sem.at[n], r_recv_sem.at[n], row=1 - r)

    def tile(first):
        at = pl.ds(pl.multiple_of(first, order), order)
        acc = jnp.zeros((order, part), jnp.float32)
        for h, (m_high, m_low) in enumerate(((high_0, low_0), (high_1, low_1))):
            both = times(m_high[at], xs[h])
            acc = acc + (both[:, :part] + both[:, part:] + times(m_low[at], xs[h, :, :part]))
        return acc

    def p_copy(n, by, b):
        return remote(
            p_send.at[n, by - 1, b], p_recv.at[n, by - 1, b],
            x_send_sem.at[n, by - 1], x_recv_sem.at[n, by - 1, b], col=col_at(by),
        )

    def multiply(n):
        s, g = n // GROUPS, n % GROUPS

        @pl.when(s == 0)
        def _():
            to_partner(hist.at[rows_of(g)], n).start()
            pl.when(has_one)(lambda: older_copy(hist.at[rows_of(g)], 0, g, 1).start())
            put(r, hist[rows_of(g)])

        @pl.when((s >= 1) & (k >= s))
        def _():
            arrived(older.at[s - 1, rows_of(g)], h_recv_sem.at[s - 1, g])
            to_partner(older.at[s - 1, rows_of(g)], n).start()
            if steps > 3:
                @pl.when((s == 1) & has_two)
                def _():
                    older_copy(older.at[0, rows_of(g)], 2, g, 2).start()
            put(r, older[s - 1, rows_of(g)])

        @pl.when((s >= 1) & (k < s))
        def _():
            to_partner(out.at[s - 1 - k, rows_of(g)], n).start()
            put(r, out[s - 1 - k, rows_of(g)])

        arrived(partner.at[n], r_recv_sem.at[n])
        put(1 - r, partner[n])

        for by in range(1, n_col):
            def far(b, carry):
                p_send[n, by - 1, b] = tile((col_at(by) * blocks + b) * order)
                p_copy(n, by, b).start()
                return carry

            lax.fori_loop(0, blocks, far, 0)

        def near(b, carry):
            total[n, b] = tile((c * blocks + b) * order)
            return carry

        lax.fori_loop(0, blocks, near, 0)

        @pl.when((s == 0) & has_two)
        def _():
            older_copy(hist.at[rows_of(g)], 1, g, 2).start()

    def z_copy(n, b):
        return remote(total.at[n, b], z_recv.at[n, b], z_send_sem.at[n], z_recv_sem.at[n, b], delay=k - 2)

    def y_copy(n, b):
        return remote(total.at[n, b], y_recv.at[n, b], z_send_sem.at[n], y_recv_sem.at[n, b], delay=k - 1)

    def b_copy(n, b, by, sem):
        s, g = n // GROUPS, n % GROUPS
        return remote(cell(s, g, b), cell(s, g, b), sem.at[n], b_recv_sem.at[n, b], delay=k + by)

    def reduce(n):
        s, g = n // GROUPS, n % GROUPS

        def one(b, carry):
            value = total[n, b]
            for by in range(1, n_col):
                arrived(p_recv.at[n, by - 1, b], x_recv_sem.at[n, by - 1, b])
                value = value + p_recv[n, by - 1, b]
            total[n, b] = value

            @pl.when(has_two)
            def _():
                arrived(z_recv.at[n, b], z_recv_sem.at[n, b])
                total[n, b] = total[n, b] + z_recv[n, b]

            pl.when(k >= 2)(lambda: z_copy(n, b).start())
            pl.when(k == 1)(lambda: y_copy(n, b).start())

            @pl.when(k == 0)
            def _():
                arrived(y_recv.at[n, b], y_recv_sem.at[n, b])
                at = pl.ds(pl.multiple_of(b * order, order), order)
                drive = sources[s, rows_of(g), at] - (total[n, b] + y_recv[n, b]).T
                out[s, rows_of(g), at] = jnp.dot(
                    drive, inverse[b], precision=lax.Precision.HIGHEST,
                    preferred_element_type=jnp.float32,
                )
                b_copy(n, b, 1, b_one_sem).start()
                if n_delay > 2:
                    b_copy(n, b, 2, b_two_sem).start()

            return carry

        lax.fori_loop(0, blocks, one, 0)

    def pass_on(n):
        s, g = n // GROUPS, n % GROUPS

        def one(b, carry):
            arrived(cell(s, g, b), b_recv_sem.at[n, b])
            pl.when(has_two)(lambda: b_copy(n, b, 2, b_two_sem).start())
            return carry

        @pl.when(k >= 1)
        def _():
            lax.fori_loop(0, blocks, one, 0)

    def turn(i, carry):
        pl.when((i >= GROUPS) & (i < items + GROUPS))(lambda: reduce(i - GROUPS))
        pl.when(i >= 2 * GROUPS)(lambda: pass_on(i - 2 * GROUPS))
        pl.when(i < items)(lambda: multiply(i))
        return carry

    lax.fori_loop(0, items + 2 * GROUPS, turn, 0)

    def whole_send(ref, sem):
        remote(ref, ref, sem, sem, row=1 - r).wait_send()

    def settle(n, carry):
        s, g = n // GROUPS, n % GROUPS
        for by in range(1, n_col):
            whole_send(p_send.at[n, by - 1], x_send_sem.at[n, by - 1])
        whole_send(partner.at[n], r_send_sem.at[n])
        pl.when(k >= 1)(lambda: whole_send(total.at[n], z_send_sem.at[n]))
        pl.when(k == 0)(lambda: whole_send(out.at[s, rows_of(g)], b_one_sem.at[n]))
        pl.when(has_two)(lambda: whole_send(out.at[s, rows_of(g)], b_two_sem.at[n]))
        return carry

    lax.fori_loop(0, items, settle, 0)
    for g in range(GROUPS):
        pl.when(has_one)(lambda: whole_send(partner.at[0], h_send_sem.at[0, g]))
        pl.when(has_two)(lambda: whole_send(partner.at[0], h_send_sem.at[1, g]))
        pl.when((k >= 1) & has_two)(lambda: whole_send(partner.at[0], h_send_sem.at[2, g]))


def on_device(n_delay, n_col, delays, history, sources, self_inverse):
    out_rows = delays.shape[1]
    halves = [delays[0, :, h, :] for h in range(2)]
    rounded = [lax.reduce_precision(half, 8, 7) for half in halves]
    highs = [x.astype(jnp.bfloat16) for x in rounded]
    lows = [(half - x).astype(jnp.bfloat16) for half, x in zip(halves, rounded)]
    steps, rows, width = sources.shape
    blocks, order, _ = self_inverse.shape
    items, part = steps * GROUPS, rows // GROUPS
    sizes = (n_delay, n_col, steps, rows, blocks, order)
    dma = pltpu.SemaphoreType.DMA
    f32 = jnp.float32
    far = n_col - 1
    cells = (items, blocks, order, part)
    return pl.pallas_call(
        functools.partial(kernel, sizes),
        out_shape=jax.ShapeDtypeStruct(sources.shape, f32),
        in_specs=[pl.BlockSpec(memory_space=pltpu.VMEM)] * 7,
        out_specs=pl.BlockSpec(memory_space=pltpu.VMEM),
        scratch_shapes=[
            pltpu.VMEM((2, width, 2 * part), jnp.bfloat16),
            pltpu.VMEM((items, part, width), f32),
            pltpu.VMEM((steps - 1, rows, width), f32),
            pltpu.VMEM((items, far, blocks, order, part), f32),
            pltpu.VMEM((items, far, blocks, order, part), f32),
            pltpu.VMEM(cells, f32),
            pltpu.VMEM(cells, f32),
            pltpu.VMEM(cells, f32),
            dma((items, far)),
            dma((items, far, blocks)),
            dma((items,)),
            dma((items, blocks)),
            dma((items, blocks)),
            dma((items,)),
            dma((items,)),
            dma((items, blocks)),
            dma((items,)),
            dma((items,)),
            dma((steps - 1, GROUPS)),
            dma((steps - 1, GROUPS)),
        ],
        compiler_params=pltpu.CompilerParams(
            collective_id=0, has_side_effects=True, vmem_limit_bytes=60 * 2**20
        ),
        cost_estimate=pl.CostEstimate(
            flops=6 * steps * rows * out_rows * 2 * width, bytes_accessed=24 * 2**20, transcendentals=0
        ),
    )(*highs, *lows, history[0], sources, self_inverse)


def solution(mesh):
    placed = (
        P("delay", "row", None, "col"),
        P("delay", None, ("row", "col")),
        P(None, None, ("row", "col")),
        P(("row", "col"), None, None),
    )
    return jax.shard_map(
        functools.partial(on_device, mesh.shape["delay"], mesh.shape["col"]),
        mesh=mesh,
        in_specs=placed,
        out_specs=P(None, None, ("row", "col")),
        check_vma=False,
    )
```

```python
import functools

import jax
import jax.numpy as jnp
from jax import lax
from jax.experimental import pallas as pl
from jax.experimental.pallas import tpu as pltpu
from jax.sharding import PartitionSpec as P

MESH = pl.DeviceIdType.MESH
GROUPS = 2


def split_two(x):
    high = x.astype(jnp.bfloat16)
    low = (x - high.astype(jnp.float32)).astype(jnp.bfloat16)
    return high, low


def times(a, b):
    return jnp.dot(a, b, preferred_element_type=jnp.float32)


def kernel(
    sizes, m_high, m_low, hist, sources, inverse, out,
    xs, partner, older, p_send, p_recv, total, z_recv, y_recv,
    x_send_sem, x_recv_sem, z_send_sem, z_recv_sem, y_recv_sem,
    b_one_sem, b_two_sem, b_recv_sem, r_send_sem, r_recv_sem, h_send_sem, h_recv_sem,
):
    n_delay, n_col, steps, rows, blocks, order = sizes
    items = steps * GROUPS
    part = rows // GROUPS
    width = blocks * order
    k = lax.axis_index("delay")
    r = lax.axis_index("row")
    c = lax.axis_index("col")
    has_one = k + 1 < n_delay
    has_two = k + 2 < n_delay

    def remote(src, dst, send, recv, **where):
        return pltpu.make_async_remote_copy(
            src_ref=src, dst_ref=dst, send_sem=send, recv_sem=recv,
            device_id=where, device_id_type=MESH,
        )

    def arrived(ref, sem):
        remote(ref, ref, sem, sem, row=1 - r).wait_recv()

    def col_at(by):
        return lax.rem(c + by, n_col)

    barrier = pltpu.get_barrier_semaphore()

    def greet(**where):
        pl.semaphore_signal(barrier, inc=1, device_id=where, device_id_type=MESH)

    greet(row=1 - r)
    for by in range(1, n_col):
        greet(col=col_at(by))
    pl.when(has_one)(lambda: greet(delay=k + 1))
    pl.when(has_two)(lambda: greet(delay=k + 2))
    pl.when(k >= 1)(lambda: greet(delay=k - 1))
    pl.when(k >= 2)(lambda: greet(delay=k - 2))
    peers = n_col
    for there in (has_one, has_two, k >= 1, k >= 2):
        peers = peers + jnp.where(there, 1, 0)
    pl.semaphore_wait(barrier, peers)

    def rows_of(g):
        return pl.ds(pl.multiple_of(g * part, part), part)

    def cell(s, g, b):
        return out.at[s, rows_of(g), pl.ds(pl.multiple_of(b * order, order), order)]

    def older_copy(src, j, g, by):
        return remote(src, older.at[j, rows_of(g)], h_send_sem.at[j, g], h_recv_sem.at[j, g], delay=k + by)

    def put(half, value):
        high, low = split_two(value.T)
        xs[half, :, :part] = high
        xs[half, :, part:] = low

    def to_partner(src, n):
        return remote(src, partner.at[n], r_send_sem.at[n], r_recv_sem.at[n], row=1 - r)

    def tile(first):
        at = pl.ds(pl.multiple_of(first, order), order)
        acc = jnp.zeros((order, part), jnp.float32)
        for h in range(2):
            here = slice(h * width, (h + 1) * width)
            both = times(m_high[at, here], xs[h])
            acc = acc + (both[:, :part] + both[:, part:] + times(m_low[at, here], xs[h, :, :part]))
        return acc

    def p_copy(n, by, b):
        return remote(
            p_send.at[n, by - 1, b], p_recv.at[n, by - 1, b],
            x_send_sem.at[n, by - 1], x_recv_sem.at[n, by - 1, b], col=col_at(by),
        )

    def multiply(n):
        s, g = n // GROUPS, n % GROUPS

        @pl.when(s == 0)
        def _():
            to_partner(hist.at[rows_of(g)], n).start()
            pl.when(has_one)(lambda: older_copy(hist.at[rows_of(g)], 0, g, 1).start())
            put(r, hist[rows_of(g)])

        @pl.when((s >= 1) & (k >= s))
        def _():
            arrived(older.at[s - 1, rows_of(g)], h_recv_sem.at[s - 1, g])
            to_partner(older.at[s - 1, rows_of(g)], n).start()
            if steps > 3:
                @pl.when((s == 1) & has_two)
                def _():
                    older_copy(older.at[0, rows_of(g)], 2, g, 2).start()
            put(r, older[s - 1, rows_of(g)])

        @pl.when((s >= 1) & (k < s))
        def _():
            to_partner(out.at[s - 1 - k, rows_of(g)], n).start()
            put(r, out[s - 1 - k, rows_of(g)])

        arrived(partner.at[n], r_recv_sem.at[n])
        put(1 - r, partner[n])

        for by in range(1, n_col):
            def far(b, carry):
                p_send[n, by - 1, b] = tile((col_at(by) * blocks + b) * order)
                p_copy(n, by, b).start()
                return carry

            lax.fori_loop(0, blocks, far, 0)

        def near(b, carry):
            total[n, b] = tile((c * blocks + b) * order)
            return carry

        lax.fori_loop(0, blocks, near, 0)

        @pl.when((s == 0) & has_two)
        def _():
            older_copy(hist.at[rows_of(g)], 1, g, 2).start()

    def z_copy(n, b):
        return remote(total.at[n, b], z_recv.at[n, b], z_send_sem.at[n], z_recv_sem.at[n, b], delay=k - 2)

    def y_copy(n, b):
        return remote(total.at[n, b], y_recv.at[n, b], z_send_sem.at[n], y_recv_sem.at[n, b], delay=k - 1)

    def b_copy(n, b, by, sem):
        s, g = n // GROUPS, n % GROUPS
        return remote(cell(s, g, b), cell(s, g, b), sem.at[n], b_recv_sem.at[n, b], delay=k + by)

    def reduce(n):
        s, g = n // GROUPS, n % GROUPS

        def one(b, carry):
            value = total[n, b]
            for by in range(1, n_col):
                arrived(p_recv.at[n, by - 1, b], x_recv_sem.at[n, by - 1, b])
                value = value + p_recv[n, by - 1, b]
            total[n, b] = value

            @pl.when(has_two)
            def _():
                arrived(z_recv.at[n, b], z_recv_sem.at[n, b])
                total[n, b] = total[n, b] + z_recv[n, b]

            pl.when(k >= 2)(lambda: z_copy(n, b).start())
            pl.when(k == 1)(lambda: y_copy(n, b).start())

            @pl.when(k == 0)
            def _():
                arrived(y_recv.at[n, b], y_recv_sem.at[n, b])
                at = pl.ds(pl.multiple_of(b * order, order), order)
                drive = sources[s, rows_of(g), at] - (total[n, b] + y_recv[n, b]).T
                out[s, rows_of(g), at] = jnp.dot(
                    drive, inverse[b], precision=lax.Precision.HIGHEST,
                    preferred_element_type=jnp.float32,
                )
                b_copy(n, b, 1, b_one_sem).start()
                if n_delay > 2:
                    b_copy(n, b, 2, b_two_sem).start()

            return carry

        lax.fori_loop(0, blocks, one, 0)

    def pass_on(n):
        s, g = n // GROUPS, n % GROUPS

        def one(b, carry):
            arrived(cell(s, g, b), b_recv_sem.at[n, b])
            pl.when(has_two)(lambda: b_copy(n, b, 2, b_two_sem).start())
            return carry

        @pl.when(k >= 1)
        def _():
            lax.fori_loop(0, blocks, one, 0)

    last = items + GROUPS
    lag = jnp.where(k < steps - 1, 2 * GROUPS, last)

    def turn(i, carry):
        pl.when((i >= GROUPS) & (i < items + GROUPS))(lambda: reduce(i - GROUPS))
        late = i - lag
        pl.when((late >= 0) & (late < items))(lambda: pass_on(late))
        pl.when(i < items)(lambda: multiply(i))
        return carry

    lax.fori_loop(0, items + last, turn, 0)

    def whole_send(ref, sem):
        remote(ref, ref, sem, sem, row=1 - r).wait_send()

    def settle(n, carry):
        s, g = n // GROUPS, n % GROUPS
        for by in range(1, n_col):
            whole_send(p_send.at[n, by - 1], x_send_sem.at[n, by - 1])
        whole_send(partner.at[n], r_send_sem.at[n])
        pl.when(k >= 1)(lambda: whole_send(total.at[n], z_send_sem.at[n]))
        pl.when(k == 0)(lambda: whole_send(out.at[s, rows_of(g)], b_one_sem.at[n]))
        pl.when(has_two)(lambda: whole_send(out.at[s, rows_of(g)], b_two_sem.at[n]))
        return carry

    lax.fori_loop(0, items, settle, 0)
    for g in range(GROUPS):
        pl.when(has_one)(lambda: whole_send(partner.at[0], h_send_sem.at[0, g]))
        pl.when(has_two)(lambda: whole_send(partner.at[0], h_send_sem.at[1, g]))
        pl.when((k >= 1) & has_two)(lambda: whole_send(partner.at[0], h_send_sem.at[2, g]))


def on_device(n_delay, n_col, delays, history, sources, self_inverse):
    out_rows = delays.shape[1]
    tiles = delays.reshape(out_rows, -1)
    rounded = lax.reduce_precision(tiles, 8, 7)
    m_high = rounded.astype(jnp.bfloat16)
    m_low = (tiles - rounded).astype(jnp.bfloat16)
    steps, rows, width = sources.shape
    blocks, order, _ = self_inverse.shape
    items, part = steps * GROUPS, rows // GROUPS
    sizes = (n_delay, n_col, steps, rows, blocks, order)
    dma = pltpu.SemaphoreType.DMA
    f32 = jnp.float32
    far = n_col - 1
    cells = (items, blocks, order, part)
    return pl.pallas_call(
        functools.partial(kernel, sizes),
        out_shape=jax.ShapeDtypeStruct(sources.shape, f32),
        in_specs=[pl.BlockSpec(memory_space=pltpu.VMEM)] * 5,
        out_specs=pl.BlockSpec(memory_space=pltpu.VMEM),
        scratch_shapes=[
            pltpu.VMEM((2, width, 2 * part), jnp.bfloat16),
            pltpu.VMEM((items, part, width), f32),
            pltpu.VMEM((steps - 1, rows, width), f32),
            pltpu.VMEM((items, far, blocks, order, part), f32),
            pltpu.VMEM((items, far, blocks, order, part), f32),
            pltpu.VMEM(cells, f32),
            pltpu.VMEM(cells, f32),
            pltpu.VMEM(cells, f32),
            dma((items, far)),
            dma((items, far, blocks)),
            dma((items,)),
            dma((items, blocks)),
            dma((items, blocks)),
            dma((items,)),
            dma((items,)),
            dma((items, blocks)),
            dma((items,)),
            dma((items,)),
            dma((steps - 1, GROUPS)),
            dma((steps - 1, GROUPS)),
        ],
        compiler_params=pltpu.CompilerParams(
            collective_id=0, has_side_effects=True, vmem_limit_bytes=60 * 2**20
        ),
        cost_estimate=pl.CostEstimate(
            flops=6 * steps * rows * out_rows * 2 * width, bytes_accessed=24 * 2**20, transcendentals=0
        ),
    )(m_high, m_low, history[0], sources, self_inverse)


def solution(mesh):
    placed = (
        P("delay", "row", None, "col"),
        P("delay", None, ("row", "col")),
        P(None, None, ("row", "col")),
        P(("row", "col"), None, None),
    )
    return jax.shard_map(
        functools.partial(on_device, mesh.shape["delay"], mesh.shape["col"]),
        mesh=mesh,
        in_specs=placed,
        out_specs=P(None, None, ("row", "col")),
        check_vma=False,
    )
```

```python
import functools

import jax
import jax.numpy as jnp
from jax import lax
from jax.experimental import pallas as pl
from jax.experimental.pallas import tpu as pltpu
from jax.sharding import PartitionSpec as P

MESH = pl.DeviceIdType.MESH
GROUPS = 2


def split_two(x):
    high = x.astype(jnp.bfloat16)
    low = (x - high.astype(jnp.float32)).astype(jnp.bfloat16)
    return high, low


def times(a, b):
    return jnp.dot(a, b, preferred_element_type=jnp.float32)


def kernel(
    sizes, m_high, m_low, hist, sources, inverse, out,
    xs, partner, older, p_send, p_recv, total, z_recv, y_recv,
    x_send_sem, x_recv_sem, z_send_sem, z_recv_sem, y_recv_sem,
    b_one_sem, b_two_sem, b_recv_sem, r_send_sem, r_recv_sem, h_send_sem, h_recv_sem,
):
    n_delay, n_col, steps, rows, blocks, order = sizes
    items = steps * GROUPS
    part = rows // GROUPS
    width = blocks * order
    k = lax.axis_index("delay")
    r = lax.axis_index("row")
    c = lax.axis_index("col")
    has_one = k + 1 < n_delay
    has_two = k + 2 < n_delay
    even = k % 2 == 0

    def remote(src, dst, send, recv, **where):
        return pltpu.make_async_remote_copy(
            src_ref=src, dst_ref=dst, send_sem=send, recv_sem=recv,
            device_id=where, device_id_type=MESH,
        )

    def arrived(ref, sem):
        remote(ref, ref, sem, sem, row=1 - r).wait_recv()

    def col_at(by):
        return lax.rem(c + by, n_col)

    barrier = pltpu.get_barrier_semaphore()

    def greet(**where):
        pl.semaphore_signal(barrier, inc=1, device_id=where, device_id_type=MESH)

    greet(row=1 - r)
    for by in range(1, n_col):
        greet(col=col_at(by))
    pl.when(has_one)(lambda: greet(delay=k + 1))
    pl.when(has_two)(lambda: greet(delay=k + 2))
    pl.when(k >= 1)(lambda: greet(delay=k - 1))
    pl.when(k >= 2)(lambda: greet(delay=k - 2))
    peers = n_col
    for there in (has_one, has_two, k >= 1, k >= 2):
        peers = peers + jnp.where(there, 1, 0)
    pl.semaphore_wait(barrier, peers)

    def rows_of(g):
        return pl.ds(pl.multiple_of(g * part, part), part)

    def cell(s, g, b):
        return out.at[s, rows_of(g), pl.ds(pl.multiple_of(b * order, order), order)]

    def older_copy(src, j, g, by):
        return remote(src, older.at[j, rows_of(g)], h_send_sem.at[j, g], h_recv_sem.at[j, g], delay=k + by)

    def put(half, value):
        high, low = split_two(value.T)
        xs[half, :, :part] = high
        xs[half, :, part:] = low

    def to_partner(src, n):
        return remote(src, partner.at[n], r_send_sem.at[n], r_recv_sem.at[n], row=1 - r)

    def tile(first):
        at = pl.ds(pl.multiple_of(first, order), order)
        acc = jnp.zeros((order, part), jnp.float32)
        for h in range(2):
            here = slice(h * width, (h + 1) * width)
            both = times(m_high[at, here], xs[h])
            acc = acc + (both[:, :part] + both[:, part:] + times(m_low[at, here], xs[h, :, :part]))
        return acc

    def p_copy(n, by, b):
        return remote(
            p_send.at[n, by - 1, b], p_recv.at[n, by - 1, b],
            x_send_sem.at[n, by - 1], x_recv_sem.at[n, by - 1, b], col=col_at(by),
        )

    def multiply(n):
        s, g = n // GROUPS, n % GROUPS

        @pl.when(s == 0)
        def _():
            to_partner(hist.at[rows_of(g)], n).start()
            pl.when(has_one)(lambda: older_copy(hist.at[rows_of(g)], 0, g, 1).start())
            put(r, hist[rows_of(g)])

        @pl.when((s >= 1) & (k >= s))
        def _():
            arrived(older.at[s - 1, rows_of(g)], h_recv_sem.at[s - 1, g])
            to_partner(older.at[s - 1, rows_of(g)], n).start()
            if steps > 3:
                @pl.when((s == 1) & has_two)
                def _():
                    older_copy(older.at[0, rows_of(g)], 2, g, 2).start()
            put(r, older[s - 1, rows_of(g)])

        @pl.when((s >= 1) & (k < s))
        def _():
            to_partner(out.at[s - 1 - k, rows_of(g)], n).start()
            put(r, out[s - 1 - k, rows_of(g)])

        arrived(partner.at[n], r_recv_sem.at[n])
        put(1 - r, partner[n])

        for by in range(1, n_col):
            def far(b, carry):
                p_send[n, by - 1, b] = tile((col_at(by) * blocks + b) * order)
                p_copy(n, by, b).start()
                return carry

            lax.fori_loop(0, blocks, far, 0)

        def near(b, carry):
            total[n, b] = tile((c * blocks + b) * order)
            return carry

        lax.fori_loop(0, blocks, near, 0)

        @pl.when((s == 0) & has_two)
        def _():
            older_copy(hist.at[rows_of(g)], 1, g, 2).start()

    def z_copy(n, b):
        return remote(total.at[n, b], z_recv.at[n, b], z_send_sem.at[n], z_recv_sem.at[n, b], delay=k - 2)

    def y_copy(n, b):
        return remote(total.at[n, b], y_recv.at[n, b], z_send_sem.at[n], y_recv_sem.at[n, b], delay=k - 1)

    def b_copy(n, b, by, sem):
        s, g = n // GROUPS, n % GROUPS
        return remote(cell(s, g, b), cell(s, g, b), sem.at[n], b_recv_sem.at[n, b], delay=k + by)

    def reduce(n):
        s, g = n // GROUPS, n % GROUPS

        def one(b, carry):
            value = total[n, b]
            for by in range(1, n_col):
                arrived(p_recv.at[n, by - 1, b], x_recv_sem.at[n, by - 1, b])
                value = value + p_recv[n, by - 1, b]
            total[n, b] = value

            @pl.when(has_two)
            def _():
                arrived(z_recv.at[n, b], z_recv_sem.at[n, b])
                total[n, b] = total[n, b] + z_recv[n, b]

            pl.when(k >= 2)(lambda: z_copy(n, b).start())
            pl.when(k == 1)(lambda: y_copy(n, b).start())

            @pl.when(k == 0)
            def _():
                arrived(y_recv.at[n, b], y_recv_sem.at[n, b])
                at = pl.ds(pl.multiple_of(b * order, order), order)
                drive = sources[s, rows_of(g), at] - (total[n, b] + y_recv[n, b]).T
                out[s, rows_of(g), at] = jnp.dot(
                    drive, inverse[b], precision=lax.Precision.HIGHEST,
                    preferred_element_type=jnp.float32,
                )
                b_copy(n, b, 1, b_one_sem).start()
                if n_delay > 2:
                    b_copy(n, b, 2, b_two_sem).start()

            return carry

        lax.fori_loop(0, blocks, one, 0)

    def pass_on(n):
        s, g = n // GROUPS, n % GROUPS

        def one(b, carry):
            arrived(cell(s, g, b), b_recv_sem.at[n, b])
            pl.when(has_two & even)(lambda: b_copy(n, b, 2, b_two_sem).start())
            pl.when(has_one & even)(lambda: b_copy(n, b, 1, b_one_sem).start())
            return carry

        @pl.when(k >= 1)
        def _():
            lax.fori_loop(0, blocks, one, 0)

    last = items + GROUPS
    lag = jnp.where(k == 0, last, jnp.where(k == 1, 4, jnp.where(k == 2, 5, jnp.where(even, 6, last))))

    def turn(i, carry):
        pl.when((i >= GROUPS) & (i < items + GROUPS))(lambda: reduce(i - GROUPS))
        late = i - lag
        pl.when((late >= 0) & (late < items))(lambda: pass_on(late))
        pl.when(i < items)(lambda: multiply(i))
        return carry

    lax.fori_loop(0, items + last, turn, 0)

    def whole_send(ref, sem):
        remote(ref, ref, sem, sem, row=1 - r).wait_send()

    def settle(n, carry):
        s, g = n // GROUPS, n % GROUPS
        for by in range(1, n_col):
            whole_send(p_send.at[n, by - 1], x_send_sem.at[n, by - 1])
        whole_send(partner.at[n], r_send_sem.at[n])
        pl.when(k >= 1)(lambda: whole_send(total.at[n], z_send_sem.at[n]))
        pl.when(has_one & even)(lambda: whole_send(out.at[s, rows_of(g)], b_one_sem.at[n]))
        pl.when(has_two & even)(lambda: whole_send(out.at[s, rows_of(g)], b_two_sem.at[n]))
        return carry

    lax.fori_loop(0, items, settle, 0)
    for g in range(GROUPS):
        pl.when(has_one)(lambda: whole_send(partner.at[0], h_send_sem.at[0, g]))
        pl.when(has_two)(lambda: whole_send(partner.at[0], h_send_sem.at[1, g]))
        pl.when((k >= 1) & has_two)(lambda: whole_send(partner.at[0], h_send_sem.at[2, g]))


def on_device(n_delay, n_col, delays, history, sources, self_inverse):
    out_rows = delays.shape[1]
    tiles = delays.reshape(out_rows, -1)
    rounded = lax.reduce_precision(tiles, 8, 7)
    m_high = rounded.astype(jnp.bfloat16)
    m_low = (tiles - rounded).astype(jnp.bfloat16)
    steps, rows, width = sources.shape
    blocks, order, _ = self_inverse.shape
    items, part = steps * GROUPS, rows // GROUPS
    sizes = (n_delay, n_col, steps, rows, blocks, order)
    dma = pltpu.SemaphoreType.DMA
    f32 = jnp.float32
    far = n_col - 1
    cells = (items, blocks, order, part)
    return pl.pallas_call(
        functools.partial(kernel, sizes),
        out_shape=jax.ShapeDtypeStruct(sources.shape, f32),
        in_specs=[pl.BlockSpec(memory_space=pltpu.VMEM)] * 5,
        out_specs=pl.BlockSpec(memory_space=pltpu.VMEM),
        scratch_shapes=[
            pltpu.VMEM((2, width, 2 * part), jnp.bfloat16),
            pltpu.VMEM((items, part, width), f32),
            pltpu.VMEM((steps - 1, rows, width), f32),
            pltpu.VMEM((items, far, blocks, order, part), f32),
            pltpu.VMEM((items, far, blocks, order, part), f32),
            pltpu.VMEM(cells, f32),
            pltpu.VMEM(cells, f32),
            pltpu.VMEM(cells, f32),
            dma((items, far)),
            dma((items, far, blocks)),
            dma((items,)),
            dma((items, blocks)),
            dma((items, blocks)),
            dma((items,)),
            dma((items,)),
            dma((items, blocks)),
            dma((items,)),
            dma((items,)),
            dma((steps - 1, GROUPS)),
            dma((steps - 1, GROUPS)),
        ],
        compiler_params=pltpu.CompilerParams(
            collective_id=0, has_side_effects=True, vmem_limit_bytes=60 * 2**20
        ),
        cost_estimate=pl.CostEstimate(
            flops=6 * steps * rows * out_rows * 2 * width, bytes_accessed=24 * 2**20, transcendentals=0
        ),
    )(m_high, m_low, history[0], sources, self_inverse)


def solution(mesh):
    placed = (
        P("delay", "row", None, "col"),
        P("delay", None, ("row", "col")),
        P(None, None, ("row", "col")),
        P(("row", "col"), None, None),
    )
    return jax.shard_map(
        functools.partial(on_device, mesh.shape["delay"], mesh.shape["col"]),
        mesh=mesh,
        in_specs=placed,
        out_specs=P(None, None, ("row", "col")),
        check_vma=False,
    )
```

```python
import functools

import jax
import jax.numpy as jnp
from jax import lax
from jax.experimental import pallas as pl
from jax.experimental.pallas import tpu as pltpu
from jax.sharding import PartitionSpec as P

MESH = pl.DeviceIdType.MESH
GROUPS = 2


def split_two(x):
    high = x.astype(jnp.bfloat16)
    low = (x - high.astype(jnp.float32)).astype(jnp.bfloat16)
    return high, low


def times(a, b):
    return jnp.dot(a, b, preferred_element_type=jnp.float32)


def kernel(
    sizes, m_high, m_low, hist, sources, inverse, out,
    xs, partner, older, p_send, p_recv, total, z_recv, y_recv,
    x_send_sem, x_recv_sem, z_send_sem, z_recv_sem, y_recv_sem,
    b_one_sem, b_two_sem, b_recv_sem, r_send_sem, r_recv_sem, h_send_sem, h_recv_sem,
):
    n_delay, n_col, steps, rows, blocks, order = sizes
    items = steps * GROUPS
    part = rows // GROUPS
    width = blocks * order
    k = lax.axis_index("delay")
    r = lax.axis_index("row")
    c = lax.axis_index("col")
    has_one = k + 1 < n_delay
    has_two = k + 2 < n_delay
    can_pair = n_col == 2 and blocks % 2 == 0 and n_delay % 2 == 0
    paired = (k >= 2) if can_pair else False
    mate = 1 - 2 * (k % 2)
    half = blocks // 2

    def remote(src, dst, send, recv, **where):
        return pltpu.make_async_remote_copy(
            src_ref=src, dst_ref=dst, send_sem=send, recv_sem=recv,
            device_id=where, device_id_type=MESH,
        )

    def arrived(ref, sem):
        remote(ref, ref, sem, sem, row=1 - r).wait_recv()

    def col_at(by):
        return lax.rem(c + by, n_col)

    barrier = pltpu.get_barrier_semaphore()

    def greet(**where):
        pl.semaphore_signal(barrier, inc=1, device_id=where, device_id_type=MESH)

    greet(row=1 - r)
    for by in range(1, n_col):
        greet(col=col_at(by))
    pl.when(has_one)(lambda: greet(delay=k + 1))
    pl.when(has_two)(lambda: greet(delay=k + 2))
    pl.when(k >= 1)(lambda: greet(delay=k - 1))
    pl.when(k >= 2)(lambda: greet(delay=k - 2))
    peers = n_col
    for there in (has_one, has_two, k >= 1, k >= 2):
        peers = peers + jnp.where(there, 1, 0)
    pl.semaphore_wait(barrier, peers)

    def rows_of(g):
        return pl.ds(pl.multiple_of(g * part, part), part)

    def cell(s, g, b):
        return out.at[s, rows_of(g), pl.ds(pl.multiple_of(b * order, order), order)]

    def older_copy(src, j, g, by):
        return remote(src, older.at[j, rows_of(g)], h_send_sem.at[j, g], h_recv_sem.at[j, g], delay=k + by)

    def put(half, value):
        high, low = split_two(value.T)
        xs[half, :, :part] = high
        xs[half, :, part:] = low

    def to_partner(src, n):
        return remote(src, partner.at[n], r_send_sem.at[n], r_recv_sem.at[n], row=1 - r)

    def tile(first):
        at = pl.ds(pl.multiple_of(first, order), order)
        acc = jnp.zeros((order, part), jnp.float32)
        for h in range(2):
            here = slice(h * width, (h + 1) * width)
            both = times(m_high[at, here], xs[h])
            acc = acc + (both[:, :part] + both[:, part:] + times(m_low[at, here], xs[h, :, :part]))
        return acc

    def p_copy(n, by, b):
        return remote(
            p_send.at[n, by - 1, b], p_recv.at[n, by - 1, b],
            x_send_sem.at[n, by - 1], x_recv_sem.at[n, by - 1, b], col=col_at(by),
        )

    def mate_copy(n, b):
        return remote(
            p_send.at[n, 0, b], y_recv.at[n, b], x_send_sem.at[n, 0], y_recv_sem.at[n, b], delay=k + mate,
        )

    def merge(n):
        def one(i, carry):
            b = i + (k % 2) * half
            arrived(y_recv.at[n, b], y_recv_sem.at[n, b])
            p_send[n, 0, b] = p_send[n, 0, b] + y_recv[n, b]
            p_copy(n, 1, b).start()
            return carry

        lax.fori_loop(0, half, one, 0)

    def multiply(n):
        s, g = n // GROUPS, n % GROUPS

        @pl.when(s == 0)
        def _():
            to_partner(hist.at[rows_of(g)], n).start()
            pl.when(has_one)(lambda: older_copy(hist.at[rows_of(g)], 0, g, 1).start())
            put(r, hist[rows_of(g)])

        @pl.when((s >= 1) & (k >= s))
        def _():
            arrived(older.at[s - 1, rows_of(g)], h_recv_sem.at[s - 1, g])
            to_partner(older.at[s - 1, rows_of(g)], n).start()
            if steps > 3:
                @pl.when((s == 1) & has_two)
                def _():
                    older_copy(older.at[0, rows_of(g)], 2, g, 2).start()
            put(r, older[s - 1, rows_of(g)])

        @pl.when((s >= 1) & (k < s))
        def _():
            to_partner(out.at[s - 1 - k, rows_of(g)], n).start()
            put(r, out[s - 1 - k, rows_of(g)])

        arrived(partner.at[n], r_recv_sem.at[n])
        put(1 - r, partner[n])

        for by in range(1, n_col):
            def far(i, carry):
                b = (i + (1 - k % 2) * half) % blocks if can_pair else i
                p_send[n, by - 1, b] = tile((col_at(by) * blocks + b) * order)
                if can_pair:
                    pl.when(jnp.logical_not(paired))(lambda: p_copy(n, by, b).start())
                    pl.when(paired & (i < half))(lambda: mate_copy(n, b).start())
                else:
                    p_copy(n, by, b).start()
                return carry

            lax.fori_loop(0, blocks, far, 0)

        def near(b, carry):
            total[n, b] = tile((c * blocks + b) * order)
            return carry

        lax.fori_loop(0, blocks, near, 0)

        @pl.when((s == 0) & has_two)
        def _():
            older_copy(hist.at[rows_of(g)], 1, g, 2).start()

    def z_copy(n, b):
        return remote(total.at[n, b], z_recv.at[n, b], z_send_sem.at[n], z_recv_sem.at[n, b], delay=k - 2)

    def y_copy(n, b):
        return remote(total.at[n, b], y_recv.at[n, b], z_send_sem.at[n], y_recv_sem.at[n, b], delay=k - 1)

    def b_copy(n, b, by, sem):
        s, g = n // GROUPS, n % GROUPS
        return remote(cell(s, g, b), cell(s, g, b), sem.at[n], b_recv_sem.at[n, b], delay=k + by)

    def reduce(n):
        s, g = n // GROUPS, n % GROUPS

        def one(b, carry):
            def take():
                value = total[n, b]
                for by in range(1, n_col):
                    arrived(p_recv.at[n, by - 1, b], x_recv_sem.at[n, by - 1, b])
                    value = value + p_recv[n, by - 1, b]
                total[n, b] = value

            if can_pair:
                pl.when(jnp.logical_not(paired) | (b // half == k % 2))(take)
            else:
                take()

            @pl.when(has_two)
            def _():
                arrived(z_recv.at[n, b], z_recv_sem.at[n, b])
                total[n, b] = total[n, b] + z_recv[n, b]

            pl.when(k >= 2)(lambda: z_copy(n, b).start())
            pl.when(k == 1)(lambda: y_copy(n, b).start())

            @pl.when(k == 0)
            def _():
                arrived(y_recv.at[n, b], y_recv_sem.at[n, b])
                at = pl.ds(pl.multiple_of(b * order, order), order)
                drive = sources[s, rows_of(g), at] - (total[n, b] + y_recv[n, b]).T
                out[s, rows_of(g), at] = jnp.dot(
                    drive, inverse[b], precision=lax.Precision.HIGHEST,
                    preferred_element_type=jnp.float32,
                )
                b_copy(n, b, 1, b_one_sem).start()
                if n_delay > 2:
                    b_copy(n, b, 2, b_two_sem).start()

            return carry

        lax.fori_loop(0, blocks, one, 0)

    def pass_on(n):
        s, g = n // GROUPS, n % GROUPS

        def one(b, carry):
            arrived(cell(s, g, b), b_recv_sem.at[n, b])
            pl.when(has_two)(lambda: b_copy(n, b, 2, b_two_sem).start())
            return carry

        @pl.when(k >= 1)
        def _():
            lax.fori_loop(0, blocks, one, 0)

    lag = jnp.where(k < 2, 2 * GROUPS, jnp.where(k < steps - 1, 3 * GROUPS, items))

    def turn(i, carry):
        if can_pair:
            pl.when(paired & (i >= 1) & (i <= items))(lambda: merge(i - 1))
        pl.when((i >= GROUPS) & (i < items + GROUPS))(lambda: reduce(i - GROUPS))
        late = i - lag
        pl.when((late >= 0) & (late < items))(lambda: pass_on(late))
        pl.when(i < items)(lambda: multiply(i))
        return carry

    lax.fori_loop(0, 2 * items, turn, 0)

    def whole_send(ref, sem):
        remote(ref, ref, sem, sem, row=1 - r).wait_send()

    def settle(n, carry):
        s, g = n // GROUPS, n % GROUPS
        for by in range(1, n_col):
            whole_send(p_send.at[n, by - 1], x_send_sem.at[n, by - 1])
        whole_send(partner.at[n], r_send_sem.at[n])
        pl.when(k >= 1)(lambda: whole_send(total.at[n], z_send_sem.at[n]))
        pl.when(k == 0)(lambda: whole_send(out.at[s, rows_of(g)], b_one_sem.at[n]))
        pl.when(has_two)(lambda: whole_send(out.at[s, rows_of(g)], b_two_sem.at[n]))
        return carry

    lax.fori_loop(0, items, settle, 0)
    for g in range(GROUPS):
        pl.when(has_one)(lambda: whole_send(partner.at[0], h_send_sem.at[0, g]))
        pl.when(has_two)(lambda: whole_send(partner.at[0], h_send_sem.at[1, g]))
        pl.when((k >= 1) & has_two)(lambda: whole_send(partner.at[0], h_send_sem.at[2, g]))


def on_device(n_delay, n_col, delays, history, sources, self_inverse):
    out_rows = delays.shape[1]
    tiles = delays.reshape(out_rows, -1)
    rounded = lax.reduce_precision(tiles, 8, 7)
    m_high = rounded.astype(jnp.bfloat16)
    m_low = (tiles - rounded).astype(jnp.bfloat16)
    steps, rows, width = sources.shape
    blocks, order, _ = self_inverse.shape
    items, part = steps * GROUPS, rows // GROUPS
    sizes = (n_delay, n_col, steps, rows, blocks, order)
    dma = pltpu.SemaphoreType.DMA
    f32 = jnp.float32
    far = n_col - 1
    cells = (items, blocks, order, part)
    return pl.pallas_call(
        functools.partial(kernel, sizes),
        out_shape=jax.ShapeDtypeStruct(sources.shape, f32),
        in_specs=[pl.BlockSpec(memory_space=pltpu.VMEM)] * 5,
        out_specs=pl.BlockSpec(memory_space=pltpu.VMEM),
        scratch_shapes=[
            pltpu.VMEM((2, width, 2 * part), jnp.bfloat16),
            pltpu.VMEM((items, part, width), f32),
            pltpu.VMEM((steps - 1, rows, width), f32),
            pltpu.VMEM((items, far, blocks, order, part), f32),
            pltpu.VMEM((items, far, blocks, order, part), f32),
            pltpu.VMEM(cells, f32),
            pltpu.VMEM(cells, f32),
            pltpu.VMEM(cells, f32),
            dma((items, far)),
            dma((items, far, blocks)),
            dma((items,)),
            dma((items, blocks)),
            dma((items, blocks)),
            dma((items,)),
            dma((items,)),
            dma((items, blocks)),
            dma((items,)),
            dma((items,)),
            dma((steps - 1, GROUPS)),
            dma((steps - 1, GROUPS)),
        ],
        compiler_params=pltpu.CompilerParams(
            collective_id=0, has_side_effects=True, vmem_limit_bytes=60 * 2**20
        ),
        cost_estimate=pl.CostEstimate(
            flops=6 * steps * rows * out_rows * 2 * width, bytes_accessed=24 * 2**20, transcendentals=0
        ),
    )(m_high, m_low, history[0], sources, self_inverse)


def solution(mesh):
    placed = (
        P("delay", "row", None, "col"),
        P("delay", None, ("row", "col")),
        P(None, None, ("row", "col")),
        P(("row", "col"), None, None),
    )
    return jax.shard_map(
        functools.partial(on_device, mesh.shape["delay"], mesh.shape["col"]),
        mesh=mesh,
        in_specs=placed,
        out_specs=P(None, None, ("row", "col")),
        check_vma=False,
    )
```

```python
import functools

import jax
import jax.numpy as jnp
from jax import lax
from jax.experimental import pallas as pl
from jax.experimental.pallas import tpu as pltpu
from jax.sharding import PartitionSpec as P

MESH = pl.DeviceIdType.MESH
GROUPS = 2


def split_two(x):
    high = x.astype(jnp.bfloat16)
    low = (x - high.astype(jnp.float32)).astype(jnp.bfloat16)
    return high, low


def times(a, b):
    return jnp.dot(a, b, preferred_element_type=jnp.float32)


def kernel(
    sizes, m_high, m_low, hist, sources, inverse, out,
    xs, partner, older, p_send, p_recv, total, z_recv, y_recv,
    x_send_sem, x_recv_sem, z_send_sem, z_recv_sem, y_recv_sem,
    b_one_sem, b_two_sem, b_recv_sem, r_send_sem, r_recv_sem, h_send_sem, h_recv_sem,
):
    n_delay, n_col, steps, rows, blocks, order = sizes
    items = steps * GROUPS
    part = rows // GROUPS
    width = blocks * order
    k = lax.axis_index("delay")
    r = lax.axis_index("row")
    c = lax.axis_index("col")
    has_one = k + 1 < n_delay
    has_two = k + 2 < n_delay
    has_four = k + 4 < n_delay
    middle = (k == 2) | (k == 3)
    above = (k == 4) | (k == 5)
    early = items // 2

    def remote(src, dst, send, recv, **where):
        return pltpu.make_async_remote_copy(
            src_ref=src, dst_ref=dst, send_sem=send, recv_sem=recv,
            device_id=where, device_id_type=MESH,
        )

    def arrived(ref, sem):
        remote(ref, ref, sem, sem, row=1 - r).wait_recv()

    def col_at(by):
        return lax.rem(c + by, n_col)

    barrier = pltpu.get_barrier_semaphore()

    def greet(**where):
        pl.semaphore_signal(barrier, inc=1, device_id=where, device_id_type=MESH)

    greet(row=1 - r)
    for by in range(1, n_col):
        greet(col=col_at(by))
    pl.when(has_one)(lambda: greet(delay=k + 1))
    pl.when(has_two)(lambda: greet(delay=k + 2))
    pl.when(k >= 1)(lambda: greet(delay=k - 1))
    pl.when(k >= 2)(lambda: greet(delay=k - 2))
    pl.when(has_four)(lambda: greet(delay=k + 4))
    pl.when(k >= 4)(lambda: greet(delay=k - 4))
    peers = n_col
    for there in (has_one, has_two, has_four, k >= 1, k >= 2, k >= 4):
        peers = peers + jnp.where(there, 1, 0)
    pl.semaphore_wait(barrier, peers)

    def rows_of(g):
        return pl.ds(pl.multiple_of(g * part, part), part)

    def cell(s, g, b):
        return out.at[s, rows_of(g), pl.ds(pl.multiple_of(b * order, order), order)]

    def older_copy(src, j, g, by):
        return remote(src, older.at[j, rows_of(g)], h_send_sem.at[j, g], h_recv_sem.at[j, g], delay=k + by)

    def put(half, value):
        high, low = split_two(value.T)
        xs[half, :, :part] = high
        xs[half, :, part:] = low

    def to_partner(src, n):
        return remote(src, partner.at[n], r_send_sem.at[n], r_recv_sem.at[n], row=1 - r)

    def tile(first):
        at = pl.ds(pl.multiple_of(first, order), order)
        acc = jnp.zeros((order, part), jnp.float32)
        for h in range(2):
            here = slice(h * width, (h + 1) * width)
            both = times(m_high[at, here], xs[h])
            acc = acc + (both[:, :part] + both[:, part:] + times(m_low[at, here], xs[h, :, :part]))
        return acc

    def p_copy(n, by, b):
        return remote(
            p_send.at[n, by - 1, b], p_recv.at[n, by - 1, b],
            x_send_sem.at[n, by - 1], x_recv_sem.at[n, by - 1, b], col=col_at(by),
        )

    def multiply(n):
        s, g = n // GROUPS, n % GROUPS

        @pl.when(s == 0)
        def _():
            to_partner(hist.at[rows_of(g)], n).start()
            pl.when(has_one)(lambda: older_copy(hist.at[rows_of(g)], 0, g, 1).start())
            put(r, hist[rows_of(g)])

        @pl.when((s >= 1) & (k >= s))
        def _():
            arrived(older.at[s - 1, rows_of(g)], h_recv_sem.at[s - 1, g])
            to_partner(older.at[s - 1, rows_of(g)], n).start()
            if steps > 3:
                @pl.when((s == 1) & has_two)
                def _():
                    older_copy(older.at[0, rows_of(g)], 2, g, 2).start()
            put(r, older[s - 1, rows_of(g)])

        @pl.when((s >= 1) & (k < s))
        def _():
            to_partner(out.at[s - 1 - k, rows_of(g)], n).start()
            put(r, out[s - 1 - k, rows_of(g)])

        arrived(partner.at[n], r_recv_sem.at[n])
        put(1 - r, partner[n])

        for by in range(1, n_col):
            def far(b, carry):
                p_send[n, by - 1, b] = tile((col_at(by) * blocks + b) * order)
                p_copy(n, by, b).start()
                return carry

            lax.fori_loop(0, blocks, far, 0)

        def near(b, carry):
            total[n, b] = tile((c * blocks + b) * order)
            return carry

        lax.fori_loop(0, blocks, near, 0)

        @pl.when((s == 0) & has_two)
        def _():
            older_copy(hist.at[rows_of(g)], 1, g, 2).start()

    def z_copy(n, b):
        return remote(total.at[n, b], z_recv.at[n, b], z_send_sem.at[n], z_recv_sem.at[n, b], delay=k - 2)

    def y_copy(n, b):
        return remote(total.at[n, b], y_recv.at[n, b], z_send_sem.at[n], y_recv_sem.at[n, b], delay=k - 1)

    def b_copy(n, b, by, sem):
        s, g = n // GROUPS, n % GROUPS
        return remote(cell(s, g, b), cell(s, g, b), sem.at[n], b_recv_sem.at[n, b], delay=k + by)

    def reduce(n):
        s, g = n // GROUPS, n % GROUPS

        def one(b, carry):
            value = total[n, b]
            for by in range(1, n_col):
                arrived(p_recv.at[n, by - 1, b], x_recv_sem.at[n, by - 1, b])
                value = value + p_recv[n, by - 1, b]
            total[n, b] = value

            @pl.when(has_two)
            def _():
                arrived(z_recv.at[n, b], z_recv_sem.at[n, b])
                total[n, b] = total[n, b] + z_recv[n, b]

            pl.when(k >= 2)(lambda: z_copy(n, b).start())
            pl.when(k == 1)(lambda: y_copy(n, b).start())

            @pl.when(k == 0)
            def _():
                arrived(y_recv.at[n, b], y_recv_sem.at[n, b])
                at = pl.ds(pl.multiple_of(b * order, order), order)
                drive = sources[s, rows_of(g), at] - (total[n, b] + y_recv[n, b]).T
                out[s, rows_of(g), at] = jnp.dot(
                    drive, inverse[b], precision=lax.Precision.HIGHEST,
                    preferred_element_type=jnp.float32,
                )
                b_copy(n, b, 1, b_one_sem).start()
                if n_delay > 2:
                    b_copy(n, b, 2, b_two_sem).start()

            return carry

        lax.fori_loop(0, blocks, one, 0)

    def pass_on(n):
        s, g = n // GROUPS, n % GROUPS

        def one(b, carry):
            arrived(cell(s, g, b), b_recv_sem.at[n, b])
            pl.when(has_two & ~(above & (n < early)))(lambda: b_copy(n, b, 2, b_two_sem).start())
            pl.when(has_four & middle & (n < early))(lambda: b_copy(n, b, 4, b_one_sem).start())
            return carry

        @pl.when(k >= 1)
        def _():
            lax.fori_loop(0, blocks, one, 0)

    last = items + GROUPS
    lag = jnp.where(k < 3, 2 * GROUPS, jnp.where(k == 3, 3 * GROUPS, last))

    def turn(i, carry):
        pl.when((i >= GROUPS) & (i < items + GROUPS))(lambda: reduce(i - GROUPS))
        late = i - lag
        pl.when((late >= 0) & (late < items))(lambda: pass_on(late))
        pl.when(i < items)(lambda: multiply(i))
        return carry

    lax.fori_loop(0, items + last, turn, 0)

    def whole_send(ref, sem):
        remote(ref, ref, sem, sem, row=1 - r).wait_send()

    def settle(n, carry):
        s, g = n // GROUPS, n % GROUPS
        for by in range(1, n_col):
            whole_send(p_send.at[n, by - 1], x_send_sem.at[n, by - 1])
        whole_send(partner.at[n], r_send_sem.at[n])
        pl.when(k >= 1)(lambda: whole_send(total.at[n], z_send_sem.at[n]))
        one_used = (k == 0) | (has_four & middle & (n < early))
        pl.when(one_used)(lambda: whole_send(out.at[s, rows_of(g)], b_one_sem.at[n]))
        two_used = has_two & ~(above & (n < early))
        pl.when(two_used)(lambda: whole_send(out.at[s, rows_of(g)], b_two_sem.at[n]))
        return carry

    lax.fori_loop(0, items, settle, 0)
    for g in range(GROUPS):
        pl.when(has_one)(lambda: whole_send(partner.at[0], h_send_sem.at[0, g]))
        pl.when(has_two)(lambda: whole_send(partner.at[0], h_send_sem.at[1, g]))
        pl.when((k >= 1) & has_two)(lambda: whole_send(partner.at[0], h_send_sem.at[2, g]))


def on_device(n_delay, n_col, delays, history, sources, self_inverse):
    out_rows = delays.shape[1]
    tiles = delays.reshape(out_rows, -1)
    rounded = lax.reduce_precision(tiles, 8, 7)
    m_high = rounded.astype(jnp.bfloat16)
    m_low = (tiles - rounded).astype(jnp.bfloat16)
    steps, rows, width = sources.shape
    blocks, order, _ = self_inverse.shape
    items, part = steps * GROUPS, rows // GROUPS
    sizes = (n_delay, n_col, steps, rows, blocks, order)
    dma = pltpu.SemaphoreType.DMA
    f32 = jnp.float32
    far = n_col - 1
    cells = (items, blocks, order, part)
    return pl.pallas_call(
        functools.partial(kernel, sizes),
        out_shape=jax.ShapeDtypeStruct(sources.shape, f32),
        in_specs=[pl.BlockSpec(memory_space=pltpu.VMEM)] * 5,
        out_specs=pl.BlockSpec(memory_space=pltpu.VMEM),
        scratch_shapes=[
            pltpu.VMEM((2, width, 2 * part), jnp.bfloat16),
            pltpu.VMEM((items, part, width), f32),
            pltpu.VMEM((steps - 1, rows, width), f32),
            pltpu.VMEM((items, far, blocks, order, part), f32),
            pltpu.VMEM((items, far, blocks, order, part), f32),
            pltpu.VMEM(cells, f32),
            pltpu.VMEM(cells, f32),
            pltpu.VMEM(cells, f32),
            dma((items, far)),
            dma((items, far, blocks)),
            dma((items,)),
            dma((items, blocks)),
            dma((items, blocks)),
            dma((items,)),
            dma((items,)),
            dma((items, blocks)),
            dma((items,)),
            dma((items,)),
            dma((steps - 1, GROUPS)),
            dma((steps - 1, GROUPS)),
        ],
        compiler_params=pltpu.CompilerParams(
            collective_id=0, has_side_effects=True, vmem_limit_bytes=60 * 2**20
        ),
        cost_estimate=pl.CostEstimate(
            flops=6 * steps * rows * out_rows * 2 * width, bytes_accessed=24 * 2**20, transcendentals=0
        ),
    )(m_high, m_low, history[0], sources, self_inverse)


def solution(mesh):
    placed = (
        P("delay", "row", None, "col"),
        P("delay", None, ("row", "col")),
        P(None, None, ("row", "col")),
        P(("row", "col"), None, None),
    )
    return jax.shard_map(
        functools.partial(on_device, mesh.shape["delay"], mesh.shape["col"]),
        mesh=mesh,
        in_specs=placed,
        out_specs=P(None, None, ("row", "col")),
        check_vma=False,
    )
```
